256 devices in a mesh: band: 8 (over z_hi, core), grid: 32 (over z_lo, y, x).
Axes of the slice: x: 4, y: 4, z: 8 (z_hi: 4, z_lo: 2; z = z_hi * 2 + z_lo), core: 2. Of those that a mesh axis runs over, the one named last changes fastest.
Arguments:
- orbitals: float32 [16, 128, 128, 128], P('band', 'grid'), may hold values from -3 to 3
- band_owner: int32 [8], replicated, may hold values from 0 to 7
- block_index: int32 [8], replicated, may hold values from 0 to 1
Outputs:
- exchange_field: float32 [16, 128, 128, 128], P('band', 'grid')
The draws below stay inside these ranges and needn't reach their ends.
All inputs are finite; a program needn't handle non-finite values.
Results may differ from the reference program's by a relative error of at most 0.0003.
Values sent between devices are 32-bit elements; how exact they have to be, the bound alone decides.
No kernel may reach another device: no remote copies, remote signals or barrier semaphores. Data moves between devices by JAX's collectives and lax.ppermute only.
A program may use at most 128 MiB of HBM per device.

```python
import math
import jax
import jax.numpy as jnp
from jax import lax

NX = 128
NY = 128
NZ = 128
HELD = 2
BLOCK = 1
ROUNDS = 8
NBANDS = 16
N_BAND = 8


def touch_ends(array, rng, smallest, largest):
    extent = array.shape
    spot = [jax.random.randint(jax.random.fold_in(rng, axis), (), 0, extent[axis]) for axis in range(len(extent))]
    array = array.at[tuple(spot)].set(smallest)
    longest = extent.index(max(extent))
    spot[longest] = (spot[longest] + 1) % extent[longest]
    return array.at[tuple(spot)].set(largest)


def block_scale(own_key, dims, shards, least, top_value):
    factor_of, own = 1.0, jax.random.fold_in(own_key, 6)
    for position, blocks in shards:
        draws = jnp.exp(jax.random.uniform(jax.random.fold_in(own, position), (blocks,), jnp.float32, least / len(shards), top_value / len(shards)))
        factor_of = factor_of * jnp.repeat(draws, dims[position] // blocks).reshape([-1 if axis == position else 1 for axis in range(len(dims))])
    return factor_of


def gaussian(rng, extent, scale, limit, cuts=(), kind=jnp.bfloat16):
    values = scale * jax.random.normal(rng, extent, jnp.float32)
    if cuts:
        values = values * block_scale(rng, extent, cuts, -0.22, 0.18)
    return jnp.clip(values, -limit, limit).astype(kind)


def setup_inputs(seed: int = 0) -> dict:
    key_of = jax.random.split(jax.random.key(seed), 4)
    return {
        "orbitals": gaussian(key_of[0], (NBANDS, NX, NY, NZ), 0.5, 3.0, ((0, 8), (1, 32)), jnp.float32),
        "band_owner": touch_ends(jax.random.randint(key_of[1], (ROUNDS,), 0, N_BAND), jax.random.fold_in(key_of[1], 1), 0, N_BAND - 1).astype(jnp.int32),
        "block_index": touch_ends(jax.random.randint(key_of[2], (ROUNDS,), 0, HELD // BLOCK), jax.random.fold_in(key_of[2], 1), 0, (HELD // BLOCK) - 1).astype(jnp.int32),
    }


CELL_EDGE = 46.9


def frequencies(length):
    index = jnp.arange(length, dtype=jnp.int32)
    return jnp.where(index < length // 2, index, index - length).astype(jnp.float32)


def coulomb_kernel(freq_x, freq_y, freq_z):
    unit_scale = (2.0 * math.pi / CELL_EDGE) ** 2
    squared = unit_scale * (freq_x[:, None, None] ** 2 + freq_y[None, :, None] ** 2 + freq_z[None, None, :] ** 2)
    guarded = jnp.where(squared > 0, squared, 1.0)
    return jnp.where(squared > 0, 4.0 * math.pi / guarded, 0.0).astype(jnp.float32)


def reference(orbitals, band_owner, block_index):
    kernel = coulomb_kernel(frequencies(NX), frequencies(NY), frequencies(NZ))
    accumulated = jnp.zeros_like(orbitals)
    for round_index in range(ROUNDS):
        offset = (band_owner[round_index] * HELD + block_index[round_index] * BLOCK).astype(jnp.int32)
        chosen = lax.dynamic_slice_in_dim(orbitals, offset, BLOCK, 0)

        def exchange_of(target):
            densities = target[None] * chosen
            spectrum = jnp.fft.fftn(densities, axes=(1, 2, 3))
            potential = jnp.real(jnp.fft.ifftn(kernel * spectrum, axes=(1, 2, 3)))
            return -jnp.sum(chosen * potential, axis=0)

        accumulated = accumulated + lax.map(exchange_of, orbitals)
    return accumulated
```

```python
import math

import jax
import jax.numpy as jnp
import numpy as np
from jax import lax
from jax.sharding import PartitionSpec as P

CELL_EDGE = 46.9
PREC = lax.Precision.HIGH


def basis(length):
    half = length // 2
    x = np.arange(length)
    rows = [np.full(length, 1.0 / math.sqrt(length))]
    rows += [math.sqrt(2.0 / length) * np.cos(2 * math.pi * (k * x % length) / length) for k in range(1, half)]
    rows += [(1.0 - 2.0 * (x % 2)) / math.sqrt(length)]
    rows += [math.sqrt(2.0 / length) * np.sin(2 * math.pi * (k * x % length) / length) for k in range(1, half)]
    freq = np.concatenate([np.arange(half + 1), np.arange(1, half)])
    return np.stack(rows).astype(np.float32), freq.astype(np.float32)


def shards(orbitals, band_owner, block_index):
    held, planes, ny, nz = orbitals.shape
    rounds = band_owner.shape[0]
    grid = lax.axis_size("grid")
    nx = planes * grid
    tx, fx = basis(nx)
    ty, fy = basis(ny)
    tz, fz = basis(nz)
    every = lax.all_gather(orbitals, "band", tiled=True)
    chosen = every[band_owner * held + block_index]
    psi = jnp.transpose(orbitals, (2, 0, 1, 3))
    chosen = jnp.transpose(chosen, (2, 0, 1, 3))
    rho = psi[:, :, None] * chosen[:, None]
    rows = held * rounds * planes
    rho = rho.reshape(ny, rows, nz)
    half = jnp.einsum("yrz,kz->yrk", rho, tz, precision=PREC)
    half = jnp.einsum("yrz,ky->krz", half, ty, precision=PREC)
    spec = lax.all_to_all(half, "grid", split_axis=0, concat_axis=0, tiled=True)
    own = ny // grid
    spec = spec.reshape(grid, own, held * rounds, planes, nz)
    txs = tx.reshape(nx, grid, planes)
    spec = jnp.einsum("sqnpz,msp->mqnz", spec, txs, precision=PREC)
    fy_own = lax.dynamic_slice_in_dim(jnp.asarray(fy), lax.axis_index("grid") * own, own)
    scale = (2.0 * math.pi / CELL_EDGE) ** 2
    squared = scale * (fx[:, None, None] ** 2 + fy_own[None, :, None] ** 2 + fz[None, None, :] ** 2)
    guarded = jnp.where(squared > 0, squared, 1.0)
    kernel = jnp.where(squared > 0, 4.0 * math.pi / guarded, 0.0)
    spec = spec * kernel[:, :, None, :]
    spec = jnp.einsum("mqnz,msp->sqnpz", spec, txs, precision=PREC)
    half = lax.all_to_all(spec.reshape(ny, rows, nz), "grid", split_axis=0, concat_axis=0, tiled=True)
    half = jnp.einsum("krz,ky->yrz", half, ty, precision=PREC)
    half = jnp.einsum("yrk,kz->yrz", half, tz, precision=PREC)
    pot = half.reshape(ny, held, rounds, planes, nz)
    out = -jnp.sum(chosen[:, None] * pot, axis=2)
    return jnp.transpose(out, (1, 2, 0, 3))


def solution(mesh):
    return jax.shard_map(
        shards,
        mesh=mesh,
        in_specs=(P("band", "grid", None, None), P(), P()),
        out_specs=P("band", "grid", None, None),
        check_vma=False,
    )
```

```python
import functools
import math

import jax
import jax.numpy as jnp
import ml_dtypes
import numpy as np
from jax import lax
from jax.experimental import pallas as pl
from jax.experimental.pallas import tpu as pltpu
from jax.sharding import PartitionSpec as P

CELL_EDGE = 46.9
GRID = "grid"


def basis(length):
    half = length // 2
    x = np.arange(length)
    rows = [np.full(length, 1.0 / math.sqrt(length))]
    rows += [math.sqrt(2.0 / length) * np.cos(2 * math.pi * (k * x % length) / length) for k in range(1, half)]
    rows += [(1.0 - 2.0 * (x % 2)) / math.sqrt(length)]
    rows += [math.sqrt(2.0 / length) * np.sin(2 * math.pi * (k * x % length) / length) for k in range(1, half)]
    freq = np.concatenate([np.arange(half + 1), np.arange(1, half)])
    return np.stack(rows), freq.astype(np.float32)


def halves(table):
    table = table.astype(np.float32)
    high = table.astype(ml_dtypes.bfloat16)
    return high, (table - high.astype(np.float32)).astype(ml_dtypes.bfloat16)


def left_table(table):
    high, low = halves(table)
    return np.block([[high, high], [low, low]])


def right_table(table):
    high, low = halves(table)
    return np.block([[high, low], [high, low]])


def split(values):
    high = values.astype(jnp.bfloat16)
    return high, (values - high.astype(jnp.float32)).astype(jnp.bfloat16)


def from_left(table, values):
    product = jnp.dot(table, jnp.concatenate(split(values), axis=0), preferred_element_type=jnp.float32)
    rows = product.shape[0] // 2
    return product[:rows] + product[rows:]


def from_right(values, table):
    product = jnp.dot(jnp.concatenate(split(values), axis=1), table, preferred_element_type=jnp.float32)
    columns = product.shape[1] // 2
    return product[:, :columns] + product[:, columns:]


def picked(core_ref, mine_ref, other_ref, plane):
    same = core_ref[pl.program_id(0)] == 0
    return jnp.where(same, mine_ref[0, plane], other_ref[0, plane])


def outward(place_ref, core_ref, own_ref, mine_ref, other_ref, wz_ref, wy_ref, out_ref):
    held, planes, ny, nz = own_ref.shape
    rows = out_ref.reshape(ny * planes * held, nz)
    for p in range(planes):
        chosen = picked(core_ref, mine_ref, other_ref, p)
        rho = jnp.concatenate([own_ref[i, p] * chosen for i in range(held)], axis=0)
        rho = from_right(rho, wz_ref[...])
        rho = jnp.concatenate([rho[i * ny:(i + 1) * ny] for i in range(held)], axis=1)
        rho = from_left(wy_ref[...], rho)
        for i in range(held):
            rows[pl.ds(p * held + i, ny, stride=planes * held), :] = rho[:, i * nz:(i + 1) * nz]


def middle(kernel_ref, wx_ref, wxi_ref, in_ref, out_ref):
    slabs, own_y, width, nz = in_ref.shape
    held = 2
    planes = width // held
    rows_in = in_ref.reshape(slabs * own_y * width, nz)
    rows_out = out_ref.reshape(slabs * own_y * width, nz)
    for q in range(own_y):
        def at(p, i):
            return pl.ds(q * width + p * held + i, slabs, stride=own_y * width)

        spec = jnp.concatenate(
            [jnp.concatenate([rows_in[at(p, i), :] for p in range(planes)], axis=0) for i in range(held)], axis=1
        )
        spec = from_left(wx_ref[...], spec)
        spec = spec * jnp.concatenate([kernel_ref[q]] * held, axis=1)
        spec = from_left(wxi_ref[...], spec)
        for i in range(held):
            for p in range(planes):
                rows_out[at(p, i), :] = spec[p * slabs:(p + 1) * slabs, i * nz:(i + 1) * nz]


def inward(place_ref, core_ref, in_ref, mine_ref, other_ref, wz_ref, wy_ref, out_ref):
    held, planes, ny, nz = out_ref.shape
    rows = in_ref.reshape(ny * planes * held, nz)

    @pl.when(pl.program_id(0) == 0)
    def _():
        out_ref[...] = jnp.zeros_like(out_ref)

    for p in range(planes):
        chosen = picked(core_ref, mine_ref, other_ref, p)
        pot = jnp.concatenate(
            [rows[pl.ds(p * held + i, ny, stride=planes * held), :] for i in range(held)], axis=1
        )
        pot = from_left(wy_ref[...], pot)
        pot = jnp.concatenate([pot[:, i * nz:(i + 1) * nz] for i in range(held)], axis=0)
        pot = from_right(pot, wz_ref[...])
        for i in range(held):
            out_ref[i, p] -= chosen * pot[i * ny:(i + 1) * ny]


def rotated(array, axis, step):
    size = lax.axis_size(axis)
    return lax.ppermute(array, axis, [(i, (i + step) % size) for i in range(size)])


def every_orbital(own):
    held = own.shape[0] // 2
    below, above = lax.optimization_barrier((rotated(own, "zh", 1), rotated(own, "zh", -1)))
    far_below = rotated(below[:held], "zh", 1)
    far_above = rotated(above[held:], "zh", -1)
    mine = jnp.concatenate([own, above, far_below, far_above, below])
    return mine, rotated(mine, "core", 1)


def whole(shape):
    return pl.BlockSpec(shape, lambda *_: (0,) * len(shape))


def shards(orbitals, band_owner, block_index):
    held, planes, ny, nz = orbitals.shape
    rounds = band_owner.shape[0]
    grid = lax.axis_size(GRID)
    nx = planes * grid
    own_y = ny // grid
    width = planes * held
    tx, fx = basis(nx)
    ty, fy = basis(ny)
    tz, fz = basis(nz)
    tx = tx.reshape(nx, grid, planes).transpose(0, 2, 1).reshape(nx, nx)
    groups, cores = lax.axis_size("zh"), lax.axis_size("core")
    place = (band_owner // cores - lax.axis_index("zh")) % groups * held + block_index
    core_off = (band_owner + lax.axis_index("core")) % cores

    fy_own = lax.dynamic_slice_in_dim(jnp.asarray(fy), lax.axis_index(GRID) * own_y, own_y)
    scale = (2.0 * math.pi / CELL_EDGE) ** 2
    squared = scale * (fx[None, :, None] ** 2 + fy_own[:, None, None] ** 2 + fz[None, None, :] ** 2)
    guarded = jnp.where(squared > 0, squared, 1.0)
    kernel = jnp.where(squared > 0, 4.0 * math.pi / guarded, 0.0)

    mine, other = every_orbital(orbitals)
    block = pl.BlockSpec((1, planes, ny, nz), lambda r, place, core: (place[r], 0, 0, 0))
    part = pl.BlockSpec((ny, width, nz), lambda r, *_: (0, r, 0))
    table = whole((2 * nz, 2 * nz))
    params = pltpu.CompilerParams(vmem_limit_bytes=48 * 2**20)
    cells = rounds * held * planes * ny * nz

    def cost(transforms):
        return pl.CostEstimate(flops=transforms * 8 * nz * cells, bytes_accessed=8 * cells, transcendentals=0)

    half = pl.pallas_call(
        outward,
        grid_spec=pltpu.PrefetchScalarGridSpec(
            num_scalar_prefetch=2,
            grid=(rounds,),
            in_specs=[whole(orbitals.shape), block, block, table, table],
            out_specs=part,
        ),
        out_shape=jax.ShapeDtypeStruct((ny, rounds * width, nz), jnp.float32),
        compiler_params=params,
        cost_estimate=cost(2),
    )(place, core_off, orbitals, mine, other, right_table(tz.T), left_table(ty))
    spec = lax.all_to_all(half, GRID, split_axis=0, concat_axis=0, tiled=True)
    strip = pl.BlockSpec((grid, own_y, width, nz), lambda r: (0, 0, r, 0))
    spec = pl.pallas_call(
        middle,
        grid=(rounds,),
        in_specs=[whole(kernel.shape), table, table, strip],
        out_specs=strip,
        out_shape=jax.ShapeDtypeStruct((grid, own_y, rounds * width, nz), jnp.float32),
        compiler_params=params,
        cost_estimate=cost(2),
    )(kernel, left_table(tx), left_table(tx.T), spec.reshape(grid, own_y, rounds * width, nz))
    half = lax.all_to_all(
        spec.reshape(ny, rounds * width, nz), GRID, split_axis=0, concat_axis=0, tiled=True
    )
    return pl.pallas_call(
        inward,
        grid_spec=pltpu.PrefetchScalarGridSpec(
            num_scalar_prefetch=2,
            grid=(rounds,),
            in_specs=[part, block, block, table, table],
            out_specs=whole(orbitals.shape),
        ),
        out_shape=jax.ShapeDtypeStruct(orbitals.shape, jnp.float32),
        compiler_params=params,
        cost_estimate=cost(2),
    )(place, core_off, half, mine, other, right_table(tz), left_table(ty.T))


def solution(mesh):
    parts = jax.sharding.Mesh(mesh.devices.reshape(4, 2, 32), ("zh", "core", GRID))
    placed = P(("zh", "core"), GRID, None, None)
    return jax.shard_map(
        shards,
        mesh=parts,
        in_specs=(placed, P(), P()),
        out_specs=placed,
        check_vma=False,
    )
```

```python
import math

import jax
import jax.numpy as jnp
import ml_dtypes
import numpy as np
from jax import lax
from jax.experimental import pallas as pl
from jax.experimental.pallas import tpu as pltpu
from jax.sharding import PartitionSpec as P

CELL_EDGE = 46.9
GRID = "grid"


def basis(length):
    half = length // 2
    x = np.arange(length)
    rows = [np.full(length, 1.0 / math.sqrt(length))]
    rows += [math.sqrt(2.0 / length) * np.cos(2 * math.pi * (k * x % length) / length) for k in range(1, half)]
    rows += [(1.0 - 2.0 * (x % 2)) / math.sqrt(length)]
    rows += [math.sqrt(2.0 / length) * np.sin(2 * math.pi * (k * x % length) / length) for k in range(1, half)]
    freq = np.concatenate([np.arange(half + 1), np.arange(1, half)])
    return np.stack(rows), freq.astype(np.float32)


def halves(table):
    table = table.astype(np.float32)
    high = table.astype(ml_dtypes.bfloat16)
    return high, (table - high.astype(np.float32)).astype(ml_dtypes.bfloat16)


def left_table(table):
    high, low = halves(table)
    return np.block([[high, high], [low, low]])


def right_table(table):
    high, low = halves(table)
    return np.block([[high, low], [high, low]])


def split(values):
    high = values.astype(jnp.bfloat16)
    return high, (values - high.astype(jnp.float32)).astype(jnp.bfloat16)


def from_left(table, values):
    product = jnp.dot(table, jnp.concatenate(split(values), axis=0), preferred_element_type=jnp.float32)
    rows = product.shape[0] // 2
    return product[:rows] + product[rows:]


def from_right(values, table):
    product = jnp.dot(jnp.concatenate(split(values), axis=1), table, preferred_element_type=jnp.float32)
    columns = product.shape[1] // 2
    return product[:, :columns] + product[:, columns:]


def outward(place_ref, core_ref, own_ref, mine_ref, other_ref, wz_ref, wy_ref, out_ref):
    held, planes, ny, nz = own_ref.shape
    width = planes * held

    def one(r, carry):
        same = core_ref[r] == 0
        place = place_ref[r]
        done = []
        for p in range(planes):
            chosen = jnp.where(same, mine_ref[place, p], other_ref[place, p])
            rho = jnp.concatenate([own_ref[i, p] * chosen for i in range(held)], axis=0)
            rho = from_right(rho, wz_ref[...])
            rho = jnp.concatenate([rho[i * ny:(i + 1) * ny] for i in range(held)], axis=1)
            rho = from_left(wy_ref[...], rho)
            done += [rho[:, i * nz:(i + 1) * nz] for i in range(held)]
        out_ref[:, pl.ds(pl.multiple_of(r * width, width), width), :] = jnp.swapaxes(jnp.stack(done), 0, 1)
        return carry

    lax.fori_loop(0, out_ref.shape[1] // width, one, 0)


def middle(kernel_ref, wx_ref, wxi_ref, in_ref, out_ref):
    slabs, own_y, step, nz = in_ref.shape
    held, planes = 2, kernel_ref.shape[1] // slabs
    width = planes * held

    def one(r, carry):
        at = pl.ds(pl.multiple_of(r * width, width), width)
        for q in range(own_y):
            spec = jnp.swapaxes(in_ref[:, q, at, :], 0, 1).reshape(planes, held, slabs, nz)
            spec = jnp.concatenate([spec[:, i].reshape(planes * slabs, nz) for i in range(held)], axis=1)
            spec = from_left(wx_ref[...], spec)
            spec = spec * jnp.concatenate([kernel_ref[q]] * held, axis=1)
            spec = from_left(wxi_ref[...], spec)
            spec = jnp.stack([spec[:, i * nz:(i + 1) * nz].reshape(planes, slabs, nz) for i in range(held)], axis=1)
            out_ref[:, q, at, :] = jnp.swapaxes(spec.reshape(width, slabs, nz), 0, 1)
        return carry

    lax.fori_loop(0, step // width, one, 0)


def inward(place_ref, core_ref, in_ref, mine_ref, other_ref, wz_ref, wy_ref, out_ref):
    held, planes, ny, nz = out_ref.shape
    width = planes * held
    out_ref[...] = jnp.zeros_like(out_ref)

    def one(r, carry):
        same = core_ref[r] == 0
        place = place_ref[r]
        pots = jnp.swapaxes(in_ref[:, pl.ds(pl.multiple_of(r * width, width), width), :], 0, 1)
        for p in range(planes):
            chosen = jnp.where(same, mine_ref[place, p], other_ref[place, p])
            pot = jnp.concatenate([pots[p * held + i] for i in range(held)], axis=1)
            pot = from_left(wy_ref[...], pot)
            pot = jnp.concatenate([pot[:, i * nz:(i + 1) * nz] for i in range(held)], axis=0)
            pot = from_right(pot, wz_ref[...])
            for i in range(held):
                out_ref[i, p] -= chosen * pot[i * ny:(i + 1) * ny]
        return carry

    lax.fori_loop(0, in_ref.shape[1] // width, one, 0)


def rotated(array, axis, step):
    size = lax.axis_size(axis)
    return lax.ppermute(array, axis, [(i, (i + step) % size) for i in range(size)])


def every_orbital(own):
    held = own.shape[0] // 2
    below, above = lax.optimization_barrier((rotated(own, "zh", 1), rotated(own, "zh", -1)))
    far_below = rotated(below[:held], "zh", 1)
    far_above = rotated(above[held:], "zh", -1)
    mine = jnp.concatenate([own, above, far_below, far_above, below])
    return mine, rotated(mine, "core", 1)


def shards(orbitals, band_owner, block_index):
    held, planes, ny, nz = orbitals.shape
    rounds = band_owner.shape[0]
    grid = lax.axis_size(GRID)
    nx = planes * grid
    own_y = ny // grid
    width = planes * held
    tx, fx = basis(nx)
    ty, fy = basis(ny)
    tz, fz = basis(nz)
    tx = tx.reshape(nx, grid, planes).transpose(0, 2, 1).reshape(nx, nx)
    groups, cores = lax.axis_size("zh"), lax.axis_size("core")
    place = (band_owner // cores - lax.axis_index("zh")) % groups * held + block_index
    core_off = (band_owner + lax.axis_index("core")) % cores

    fy_own = lax.dynamic_slice_in_dim(jnp.asarray(fy), lax.axis_index(GRID) * own_y, own_y)
    scale = (2.0 * math.pi / CELL_EDGE) ** 2
    squared = scale * (fx[None, :, None] ** 2 + fy_own[:, None, None] ** 2 + fz[None, None, :] ** 2)
    guarded = jnp.where(squared > 0, squared, 1.0)
    kernel = jnp.where(squared > 0, 4.0 * math.pi / guarded, 0.0)

    mine, other = every_orbital(orbitals)
    kernel, other = lax.optimization_barrier((kernel, other))
    cells = rounds * held * planes * ny * nz
    vmem, smem = pl.BlockSpec(memory_space=pltpu.VMEM), pl.BlockSpec(memory_space=pltpu.SMEM)

    def call(body, shape, scalars, operands):
        return pl.pallas_call(
            body,
            in_specs=[smem] * len(scalars) + [vmem] * len(operands),
            out_specs=vmem,
            out_shape=jax.ShapeDtypeStruct(shape, jnp.float32),
            compiler_params=pltpu.CompilerParams(vmem_limit_bytes=24 * 2**20),
            cost_estimate=pl.CostEstimate(flops=16 * nz * cells, bytes_accessed=8 * cells, transcendentals=0),
        )(*scalars, *operands)

    scalars = (place, core_off)
    half = call(
        outward, (ny, rounds * width, nz), scalars, (orbitals, mine, other, right_table(tz.T), left_table(ty))
    )
    spec = lax.all_to_all(half, GRID, split_axis=0, concat_axis=0, tiled=True)
    strips = (grid, own_y, rounds * width, nz)
    spec = call(middle, strips, (), (kernel, left_table(tx), left_table(tx.T), spec.reshape(strips)))
    half = lax.all_to_all(
        spec.reshape(ny, rounds * width, nz), GRID, split_axis=0, concat_axis=0, tiled=True
    )
    return call(inward, orbitals.shape, scalars, (half, mine, other, right_table(tz), left_table(ty.T)))


def solution(mesh):
    parts = jax.sharding.Mesh(mesh.devices.reshape(4, 2, 32), ("zh", "core", GRID))
    placed = P(("zh", "core"), GRID, None, None)
    return jax.shard_map(
        shards,
        mesh=parts,
        in_specs=(placed, P(), P()),
        out_specs=placed,
        check_vma=False,
    )
```

```python
import math

import jax
import jax.numpy as jnp
import ml_dtypes
import numpy as np
from jax import lax
from jax.experimental import pallas as pl
from jax.experimental.pallas import tpu as pltpu
from jax.sharding import PartitionSpec as P

CELL_EDGE = 46.9
GRID = "grid"
UNROLL = 8


def basis(length):
    half = length // 2
    x = np.arange(length)
    rows = [np.full(length, 1.0 / math.sqrt(length))]
    rows += [math.sqrt(2.0 / length) * np.cos(2 * math.pi * (k * x % length) / length) for k in range(1, half)]
    rows += [(1.0 - 2.0 * (x % 2)) / math.sqrt(length)]
    rows += [math.sqrt(2.0 / length) * np.sin(2 * math.pi * (k * x % length) / length) for k in range(1, half)]
    freq = np.concatenate([np.arange(half + 1), np.arange(1, half)])
    return np.stack(rows), freq.astype(np.float32)


def halves(table):
    table = table.astype(np.float32)
    high = table.astype(ml_dtypes.bfloat16)
    return high, (table - high.astype(np.float32)).astype(ml_dtypes.bfloat16)


def left_table(table):
    high, low = halves(table)
    return np.block([[high, high], [low, low]])


def right_table(table):
    high, low = halves(table)
    return np.block([[high, low], [high, low]])


def split(values):
    high = values.astype(jnp.bfloat16)
    return high, (values - high.astype(jnp.float32)).astype(jnp.bfloat16)


def from_left(table, values):
    product = jnp.dot(table, jnp.concatenate(split(values), axis=0), preferred_element_type=jnp.float32)
    rows = product.shape[0] // 2
    return product[:rows] + product[rows:]


def from_right(values, table):
    product = jnp.dot(jnp.concatenate(split(values), axis=1), table, preferred_element_type=jnp.float32)
    columns = product.shape[1] // 2
    return product[:, :columns] + product[:, columns:]


def outward(place_ref, core_ref, own_ref, mine_ref, other_ref, wz_ref, wy_ref, out_ref, chosen_ref):
    held, planes, ny, nz = own_ref.shape
    width = planes * held

    def one(r, carry):
        same = core_ref[r] == 0
        place = place_ref[r]
        done = []
        for p in range(planes):
            chosen = jnp.where(same, mine_ref[place, p], other_ref[place, p])
            chosen_ref[r, p] = chosen
            rho = jnp.concatenate([own_ref[i, p] * chosen for i in range(held)], axis=0)
            rho = from_right(rho, wz_ref[...])
            rho = jnp.concatenate([rho[i * ny:(i + 1) * ny] for i in range(held)], axis=1)
            rho = from_left(wy_ref[...], rho)
            done += [rho[:, i * nz:(i + 1) * nz] for i in range(held)]
        out_ref[:, pl.ds(pl.multiple_of(r * width, width), width), :] = jnp.swapaxes(jnp.stack(done), 0, 1)
        return carry

    lax.fori_loop(0, out_ref.shape[1] // width, one, 0, unroll=UNROLL)


def middle(kernel_ref, wx_ref, wxi_ref, in_ref, out_ref):
    slabs, own_y, step, nz = in_ref.shape
    held, planes = 2, kernel_ref.shape[1] // slabs
    width = planes * held

    def one(r, carry):
        at = pl.ds(pl.multiple_of(r * width, width), width)
        for q in range(own_y):
            spec = jnp.swapaxes(in_ref[:, q, at, :], 0, 1).reshape(planes, held, slabs, nz)
            spec = jnp.concatenate([spec[:, i].reshape(planes * slabs, nz) for i in range(held)], axis=1)
            spec = from_left(wx_ref[...], spec)
            spec = spec * jnp.concatenate([kernel_ref[q]] * held, axis=1)
            spec = from_left(wxi_ref[...], spec)
            spec = jnp.stack([spec[:, i * nz:(i + 1) * nz].reshape(planes, slabs, nz) for i in range(held)], axis=1)
            out_ref[:, q, at, :] = jnp.swapaxes(spec.reshape(width, slabs, nz), 0, 1)
        return carry

    lax.fori_loop(0, step // width, one, 0, unroll=UNROLL)


def inward(in_ref, chosen_ref, wz_ref, wy_ref, out_ref):
    held, planes, ny, nz = out_ref.shape
    width = planes * held
    out_ref[...] = jnp.zeros_like(out_ref)

    def one(r, carry):
        pots = jnp.swapaxes(in_ref[:, pl.ds(pl.multiple_of(r * width, width), width), :], 0, 1)
        for p in range(planes):
            pot = jnp.concatenate([pots[p * held + i] for i in range(held)], axis=1)
            pot = from_left(wy_ref[...], pot)
            pot = jnp.concatenate([pot[:, i * nz:(i + 1) * nz] for i in range(held)], axis=0)
            pot = from_right(pot, wz_ref[...])
            for i in range(held):
                out_ref[i, p] -= chosen_ref[r, p] * pot[i * ny:(i + 1) * ny]
        return carry

    lax.fori_loop(0, in_ref.shape[1] // width, one, 0, unroll=UNROLL)


def rotated(array, axis, step):
    size = lax.axis_size(axis)
    return lax.ppermute(array, axis, [(i, (i + step) % size) for i in range(size)])


def every_orbital(own):
    held = own.shape[0] // 2
    below, above = lax.optimization_barrier((rotated(own, "zh", 1), rotated(own, "zh", -1)))
    far_below = rotated(below[:held], "zh", 1)
    far_above = rotated(above[held:], "zh", -1)
    mine = jnp.concatenate([own, above, far_below, far_above, below])
    return mine, rotated(mine, "core", 1)


def shards(orbitals, band_owner, block_index):
    held, planes, ny, nz = orbitals.shape
    rounds = band_owner.shape[0]
    grid = lax.axis_size(GRID)
    nx = planes * grid
    own_y = ny // grid
    width = planes * held
    tx, fx = basis(nx)
    ty, fy = basis(ny)
    tz, fz = basis(nz)
    order = np.arange(grid).reshape(-1, 4, 4).transpose(2, 1, 0).reshape(grid)
    tx = tx.reshape(nx, grid, planes)[:, order].transpose(0, 2, 1).reshape(nx, nx)
    groups, cores = lax.axis_size("zh"), lax.axis_size("core")
    place = (band_owner // cores - lax.axis_index("zh")) % groups * held + block_index
    core_off = (band_owner + lax.axis_index("core")) % cores

    spot = jnp.asarray(np.argsort(order).astype(np.int32))[lax.axis_index(GRID)]
    fy_own = lax.dynamic_slice_in_dim(jnp.asarray(fy), spot * own_y, own_y)
    scale = (2.0 * math.pi / CELL_EDGE) ** 2
    squared = scale * (fx[None, :, None] ** 2 + fy_own[:, None, None] ** 2 + fz[None, None, :] ** 2)
    guarded = jnp.where(squared > 0, squared, 1.0)
    kernel = jnp.where(squared > 0, 4.0 * math.pi / guarded, 0.0)

    mine, other = every_orbital(orbitals)
    kernel, other = lax.optimization_barrier((kernel, other))
    cells = rounds * held * planes * ny * nz
    vmem, smem = pl.BlockSpec(memory_space=pltpu.VMEM), pl.BlockSpec(memory_space=pltpu.SMEM)

    def call(body, shapes, scalars, operands):
        return pl.pallas_call(
            body,
            in_specs=[smem] * len(scalars) + [vmem] * len(operands),
            out_specs=[vmem] * len(shapes),
            out_shape=[jax.ShapeDtypeStruct(shape, jnp.float32) for shape in shapes],
            compiler_params=pltpu.CompilerParams(vmem_limit_bytes=16 * 2**20),
            cost_estimate=pl.CostEstimate(flops=16 * nz * cells, bytes_accessed=8 * cells, transcendentals=0),
        )(*scalars, *operands)

    def exchange(array):
        return lax.all_to_all(
            array, GRID, split_axis=0, concat_axis=0, tiled=True, axis_index_groups=[order.tolist()]
        )

    sent = (ny, rounds * width, nz)
    half, chosen = call(
        outward,
        [sent, (rounds, planes, ny, nz)],
        (place, core_off),
        (orbitals, mine, other, right_table(tz.T), left_table(ty)),
    )
    strips = (grid, own_y, rounds * width, nz)
    spec = exchange(half).reshape(strips)
    (spec,) = call(middle, [strips], (), (kernel, left_table(tx), left_table(tx.T), spec))
    half = exchange(spec.reshape(sent))
    (out,) = call(inward, [orbitals.shape], (), (half, chosen, right_table(tz), left_table(ty.T)))
    return out


def solution(mesh):
    parts = jax.sharding.Mesh(mesh.devices.reshape(4, 2, 32), ("zh", "core", GRID))
    placed = P(("zh", "core"), GRID, None, None)
    return jax.shard_map(
        shards,
        mesh=parts,
        in_specs=(placed, P(), P()),
        out_specs=placed,
        check_vma=False,
    )
```

```python
import math

import jax
import jax.numpy as jnp
import ml_dtypes
import numpy as np
from jax import lax
from jax.experimental import pallas as pl
from jax.experimental.pallas import tpu as pltpu
from jax.sharding import PartitionSpec as P

CELL_EDGE = 46.9
GRID = "grid"
UNROLL = 8


def basis(length):
    half = length // 2
    x = np.arange(length)
    rows = [np.full(length, 1.0 / math.sqrt(length))]
    rows += [math.sqrt(2.0 / length) * np.cos(2 * math.pi * (k * x % length) / length) for k in range(1, half)]
    rows += [(1.0 - 2.0 * (x % 2)) / math.sqrt(length)]
    rows += [math.sqrt(2.0 / length) * np.sin(2 * math.pi * (k * x % length) / length) for k in range(1, half)]
    freq = np.concatenate([np.arange(half + 1), np.arange(1, half)])
    return np.stack(rows), freq.astype(np.float32)


def halves(table):
    table = table.astype(np.float32)
    high = table.astype(ml_dtypes.bfloat16)
    return high, (table - high.astype(np.float32)).astype(ml_dtypes.bfloat16)


def left_table(table):
    high, low = halves(table)
    return np.block([[high, high], [low, low]])


def right_table(table):
    high, low = halves(table)
    return np.block([[high, low], [high, low]])


def split(values):
    high = values.astype(jnp.bfloat16)
    return high, (values - high.astype(jnp.float32)).astype(jnp.bfloat16)


def from_left(table, values):
    product = jnp.dot(table, jnp.concatenate(split(values), axis=0), preferred_element_type=jnp.float32)
    rows = product.shape[0] // 2
    return product[:rows] + product[rows:]


def from_right(values, table):
    product = jnp.dot(jnp.concatenate(split(values), axis=1), table, preferred_element_type=jnp.float32)
    columns = product.shape[1] // 2
    return product[:, :columns] + product[:, columns:]


def outward(place_ref, core_ref, own_ref, mine_ref, other_ref, wz_ref, wy_ref, out_ref, chosen_ref):
    held, planes, ny, nz = own_ref.shape
    width = planes * held

    def one(r, carry):
        same = core_ref[r] == 0
        place = place_ref[r]
        done = []
        for p in range(planes):
            chosen = jnp.where(same, mine_ref[place, p], other_ref[place, p])
            chosen_ref[r, p] = chosen
            rho = jnp.concatenate([own_ref[i, p] * chosen for i in range(held)], axis=0)
            rho = from_right(rho, wz_ref[...])
            rho = jnp.concatenate([rho[i * ny:(i + 1) * ny] for i in range(held)], axis=1)
            rho = from_left(wy_ref[...], rho)
            done += [rho[:, i * nz:(i + 1) * nz] for i in range(held)]
        out_ref[:, pl.ds(pl.multiple_of(r * width, width), width), :] = jnp.swapaxes(jnp.stack(done), 0, 1)
        return carry

    lax.fori_loop(0, out_ref.shape[1] // width, one, 0, unroll=UNROLL)


def middle(kernel_ref, wx_ref, wxi_ref, in_ref, out_ref):
    slabs, own_y, step, nz = in_ref.shape
    held, planes = 2, kernel_ref.shape[1] // slabs
    width = planes * held

    def one(r, carry):
        at = pl.ds(pl.multiple_of(r * width, width), width)
        for q in range(own_y):
            spec = jnp.swapaxes(in_ref[:, q, at, :], 0, 1).reshape(planes, held, slabs, nz)
            spec = jnp.concatenate([spec[:, i].reshape(planes * slabs, nz) for i in range(held)], axis=1)
            spec = from_left(wx_ref[...], spec)
            spec = spec * jnp.concatenate([kernel_ref[q]] * held, axis=1)
            spec = from_left(wxi_ref[...], spec)
            spec = jnp.stack([spec[:, i * nz:(i + 1) * nz].reshape(planes, slabs, nz) for i in range(held)], axis=1)
            out_ref[:, q, at, :] = jnp.swapaxes(spec.reshape(width, slabs, nz), 0, 1)
        return carry

    lax.fori_loop(0, step // width, one, 0, unroll=UNROLL)


def inward(in_ref, chosen_ref, wz_ref, wy_ref, out_ref):
    held, planes, ny, nz = out_ref.shape
    width = planes * held
    out_ref[...] = jnp.zeros_like(out_ref)

    def one(r, carry):
        pots = jnp.swapaxes(in_ref[:, pl.ds(pl.multiple_of(r * width, width), width), :], 0, 1)
        for p in range(planes):
            pot = jnp.concatenate([pots[p * held + i] for i in range(held)], axis=1)
            pot = from_left(wy_ref[...], pot)
            pot = jnp.concatenate([pot[:, i * nz:(i + 1) * nz] for i in range(held)], axis=0)
            pot = from_right(pot, wz_ref[...])
            for i in range(held):
                out_ref[i, p] -= chosen_ref[r, p] * pot[i * ny:(i + 1) * ny]
        return carry

    lax.fori_loop(0, in_ref.shape[1] // width, one, 0, unroll=UNROLL)


def rotated(array, axis, step):
    size = lax.axis_size(axis)
    return lax.ppermute(array, axis, [(i, (i + step) % size) for i in range(size)])


def every_orbital(own):
    held = own.shape[0] // 2
    first, last = own[:held], own[held:]
    below_first, above_last = rotated(first, "zh", 1), rotated(last, "zh", -1)
    below_last, above_first = rotated(last, "zh", 1), rotated(first, "zh", -1)
    far_first, far_last = rotated(below_first, "zh", 1), rotated(above_last, "zh", -1)
    mine = jnp.concatenate(
        [own, above_first, above_last, far_first, far_last, below_first, below_last]
    )
    return mine, rotated(mine, "core", 1)


def shards(orbitals, band_owner, block_index):
    held, planes, ny, nz = orbitals.shape
    rounds = band_owner.shape[0]
    grid = lax.axis_size(GRID)
    nx = planes * grid
    own_y = ny // grid
    width = planes * held
    tx, fx = basis(nx)
    ty, fy = basis(ny)
    tz, fz = basis(nz)
    order = np.arange(grid).reshape(-1, 4, 4).transpose(2, 1, 0).reshape(grid)
    tx = tx.reshape(nx, grid, planes)[:, order].transpose(0, 2, 1).reshape(nx, nx)
    groups, cores = lax.axis_size("zh"), lax.axis_size("core")
    place = (band_owner // cores - lax.axis_index("zh")) % groups * held + block_index
    core_off = (band_owner + lax.axis_index("core")) % cores

    spot = jnp.asarray(np.argsort(order).astype(np.int32))[lax.axis_index(GRID)]
    fy_own = lax.dynamic_slice_in_dim(jnp.asarray(fy), spot * own_y, own_y)
    scale = (2.0 * math.pi / CELL_EDGE) ** 2
    squared = scale * (fx[None, :, None] ** 2 + fy_own[:, None, None] ** 2 + fz[None, None, :] ** 2)
    guarded = jnp.where(squared > 0, squared, 1.0)
    kernel = jnp.where(squared > 0, 4.0 * math.pi / guarded, 0.0)

    mine, other = every_orbital(orbitals)
    kernel, other = lax.optimization_barrier((kernel, other))
    cells = rounds * held * planes * ny * nz
    vmem, smem = pl.BlockSpec(memory_space=pltpu.VMEM), pl.BlockSpec(memory_space=pltpu.SMEM)

    def call(body, shapes, scalars, operands):
        return pl.pallas_call(
            body,
            in_specs=[smem] * len(scalars) + [vmem] * len(operands),
            out_specs=[vmem] * len(shapes),
            out_shape=[jax.ShapeDtypeStruct(shape, jnp.float32) for shape in shapes],
            compiler_params=pltpu.CompilerParams(vmem_limit_bytes=16 * 2**20),
            cost_estimate=pl.CostEstimate(flops=16 * nz * cells, bytes_accessed=8 * cells, transcendentals=0),
        )(*scalars, *operands)

    def exchange(array):
        return lax.all_to_all(
            array, GRID, split_axis=0, concat_axis=0, tiled=True, axis_index_groups=[order.tolist()]
        )

    sent = (ny, rounds * width, nz)
    half, chosen = call(
        outward,
        [sent, (rounds, planes, ny, nz)],
        (place, core_off),
        (orbitals, mine, other, right_table(tz.T), left_table(ty)),
    )
    strips = (grid, own_y, rounds * width, nz)
    spec = exchange(half).reshape(strips)
    (spec,) = call(middle, [strips], (), (kernel, left_table(tx), left_table(tx.T), spec))
    half = exchange(spec.reshape(sent))
    (out,) = call(inward, [orbitals.shape], (), (half, chosen, right_table(tz), left_table(ty.T)))
    return out


def solution(mesh):
    parts = jax.sharding.Mesh(mesh.devices.reshape(4, 2, 32), ("zh", "core", GRID))
    placed = P(("zh", "core"), GRID, None, None)
    return jax.shard_map(
        shards,
        mesh=parts,
        in_specs=(placed, P(), P()),
        out_specs=placed,
        check_vma=False,
    )
```

```python
import math

import jax
import jax.numpy as jnp
import ml_dtypes
import numpy as np
from jax import lax
from jax.experimental import pallas as pl
from jax.experimental.pallas import tpu as pltpu
from jax.sharding import PartitionSpec as P

CELL_EDGE = 46.9
GRID = "grid"
UNROLL = 8


def basis(length):
    half = length // 2
    x = np.arange(length)
    rows = [np.full(length, 1.0 / math.sqrt(length))]
    rows += [math.sqrt(2.0 / length) * np.cos(2 * math.pi * (k * x % length) / length) for k in range(1, half)]
    rows += [(1.0 - 2.0 * (x % 2)) / math.sqrt(length)]
    rows += [math.sqrt(2.0 / length) * np.sin(2 * math.pi * (k * x % length) / length) for k in range(1, half)]
    freq = np.concatenate([np.arange(half + 1), np.arange(1, half)])
    return np.stack(rows), freq.astype(np.float32)


def halves(table):
    table = table.astype(np.float32)
    high = table.astype(ml_dtypes.bfloat16)
    return high, (table - high.astype(np.float32)).astype(ml_dtypes.bfloat16)


def left_table(table):
    high, low = halves(table)
    return np.block([[high, high], [low, low]])


def right_table(table):
    high, low = halves(table)
    return np.block([[high, low], [high, low]])


def split(values):
    high = values.astype(jnp.bfloat16)
    return high, (values - high.astype(jnp.float32)).astype(jnp.bfloat16)


def from_left(table, values):
    product = jnp.dot(table, jnp.concatenate(split(values), axis=0), preferred_element_type=jnp.float32)
    rows = product.shape[0] // 2
    return product[:rows] + product[rows:]


def from_right(values, table):
    product = jnp.dot(jnp.concatenate(split(values), axis=1), table, preferred_element_type=jnp.float32)
    columns = product.shape[1] // 2
    return product[:, :columns] + product[:, columns:]


def outward(place_ref, core_ref, own_ref, mine_ref, other_ref, wz_ref, wy_ref, out_ref, chosen_ref):
    held, planes, ny, nz = own_ref.shape
    width = planes * held

    def one(r, carry):
        same = core_ref[r] == 0
        place = place_ref[r]
        done = []
        for p in range(planes):
            chosen = jnp.where(same, mine_ref[place, p], other_ref[place, p])
            chosen_ref[r, p] = chosen
            rho = jnp.concatenate([own_ref[i, p] * chosen for i in range(held)], axis=0)
            rho = from_right(rho, wz_ref[...])
            rho = jnp.concatenate([rho[i * ny:(i + 1) * ny] for i in range(held)], axis=1)
            rho = from_left(wy_ref[...], rho)
            done += [rho[:, i * nz:(i + 1) * nz] for i in range(held)]
        out_ref[:, pl.ds(pl.multiple_of(r * width, width), width), :] = jnp.swapaxes(jnp.stack(done), 0, 1)
        return carry

    lax.fori_loop(0, out_ref.shape[1] // width, one, 0, unroll=UNROLL)


def middle(kernel_ref, wx_ref, wxi_ref, in_ref, out_ref):
    slabs, own_y, step, nz = in_ref.shape
    held, planes = 2, kernel_ref.shape[1] // slabs
    width = planes * held

    def one(r, carry):
        at = pl.ds(pl.multiple_of(r * width, width), width)
        for q in range(own_y):
            spec = jnp.swapaxes(in_ref[:, q, at, :], 0, 1).reshape(planes, held, slabs, nz)
            spec = jnp.concatenate([spec[:, i].reshape(planes * slabs, nz) for i in range(held)], axis=1)
            spec = from_left(wx_ref[...], spec)
            spec = spec * jnp.concatenate([kernel_ref[q]] * held, axis=1)
            spec = from_left(wxi_ref[...], spec)
            spec = jnp.stack([spec[:, i * nz:(i + 1) * nz].reshape(planes, slabs, nz) for i in range(held)], axis=1)
            out_ref[:, q, at, :] = jnp.swapaxes(spec.reshape(width, slabs, nz), 0, 1)
        return carry

    lax.fori_loop(0, step // width, one, 0, unroll=UNROLL)


def inward(in_ref, chosen_ref, wz_ref, wy_ref, out_ref):
    held, planes, ny, nz = out_ref.shape
    width = planes * held
    out_ref[...] = jnp.zeros_like(out_ref)

    def one(r, carry):
        pots = jnp.swapaxes(in_ref[:, pl.ds(pl.multiple_of(r * width, width), width), :], 0, 1)
        for p in range(planes):
            pot = jnp.concatenate([pots[p * held + i] for i in range(held)], axis=1)
            pot = from_left(wy_ref[...], pot)
            pot = jnp.concatenate([pot[:, i * nz:(i + 1) * nz] for i in range(held)], axis=0)
            pot = from_right(pot, wz_ref[...])
            for i in range(held):
                out_ref[i, p] -= chosen_ref[r, p] * pot[i * ny:(i + 1) * ny]
        return carry

    lax.fori_loop(0, in_ref.shape[1] // width, one, 0, unroll=UNROLL)


def rotated(array, axis, step):
    size = lax.axis_size(axis)
    return lax.ppermute(array, axis, [(i, (i + step) % size) for i in range(size)])


def every_orbital(own):
    held = own.shape[0] // 2
    first, last = own[:held], own[held:]
    below_first, above_last = rotated(first, "zh", 1), rotated(last, "zh", -1)
    below_last, above_first = rotated(last, "zh", 1), rotated(first, "zh", -1)
    far_first, far_last = rotated(below_first, "zh", 1), rotated(above_last, "zh", -1)
    blocks = [below_first, below_last, above_first, above_last]
    blocks.append(jnp.concatenate([far_first, far_last, own]))
    return jnp.concatenate(blocks), jnp.concatenate([rotated(block, "core", 1) for block in blocks])


def shards(orbitals, band_owner, block_index):
    held, planes, ny, nz = orbitals.shape
    rounds = band_owner.shape[0]
    grid = lax.axis_size(GRID)
    nx = planes * grid
    own_y = ny // grid
    width = planes * held
    tx, fx = basis(nx)
    ty, fy = basis(ny)
    tz, fz = basis(nz)
    order = np.arange(grid).reshape(-1, 4, 4).transpose(2, 1, 0).reshape(grid)
    tx = tx.reshape(nx, grid, planes)[:, order].transpose(0, 2, 1).reshape(nx, nx)
    groups, cores = lax.axis_size("zh"), lax.axis_size("core")
    offset = (band_owner // cores - lax.axis_index("zh")) % groups
    place = jnp.where(offset == 0, groups - 1, jnp.where(offset == groups - 1, 0, offset)) * held + block_index
    core_off = (band_owner + lax.axis_index("core")) % cores

    spot = jnp.asarray(np.argsort(order).astype(np.int32))[lax.axis_index(GRID)]
    fy_own = lax.dynamic_slice_in_dim(jnp.asarray(fy), spot * own_y, own_y)
    scale = (2.0 * math.pi / CELL_EDGE) ** 2
    squared = scale * (fx[None, :, None] ** 2 + fy_own[:, None, None] ** 2 + fz[None, None, :] ** 2)
    guarded = jnp.where(squared > 0, squared, 1.0)
    kernel = jnp.where(squared > 0, 4.0 * math.pi / guarded, 0.0)

    mine, other = every_orbital(orbitals)
    kernel, other = lax.optimization_barrier((kernel, other))
    cells = rounds * held * planes * ny * nz
    vmem, smem = pl.BlockSpec(memory_space=pltpu.VMEM), pl.BlockSpec(memory_space=pltpu.SMEM)

    def call(body, shapes, scalars, operands):
        return pl.pallas_call(
            body,
            in_specs=[smem] * len(scalars) + [vmem] * len(operands),
            out_specs=[vmem] * len(shapes),
            out_shape=[jax.ShapeDtypeStruct(shape, jnp.float32) for shape in shapes],
            compiler_params=pltpu.CompilerParams(vmem_limit_bytes=16 * 2**20),
            cost_estimate=pl.CostEstimate(flops=16 * nz * cells, bytes_accessed=8 * cells, transcendentals=0),
        )(*scalars, *operands)

    def exchange(array):
        return lax.all_to_all(
            array, GRID, split_axis=0, concat_axis=0, tiled=True, axis_index_groups=[order.tolist()]
        )

    sent = (ny, rounds * width, nz)
    half, chosen = call(
        outward,
        [sent, (rounds, planes, ny, nz)],
        (place, core_off),
        (orbitals, mine, other, right_table(tz.T), left_table(ty)),
    )
    strips = (grid, own_y, rounds * width, nz)
    spec = exchange(half).reshape(strips)
    (spec,) = call(middle, [strips], (), (kernel, left_table(tx), left_table(tx.T), spec))
    half = exchange(spec.reshape(sent))
    (out,) = call(inward, [orbitals.shape], (), (half, chosen, right_table(tz), left_table(ty.T)))
    return out


def solution(mesh):
    parts = jax.sharding.Mesh(mesh.devices.reshape(4, 2, 32), ("zh", "core", GRID))
    placed = P(("zh", "core"), GRID, None, None)
    return jax.shard_map(
        shards,
        mesh=parts,
        in_specs=(placed, P(), P()),
        out_specs=placed,
        check_vma=False,
    )
```

```python
import math

import jax
import jax.numpy as jnp
import ml_dtypes
import numpy as np
from jax import lax
from jax.experimental import pallas as pl
from jax.experimental.pallas import tpu as pltpu
from jax.sharding import PartitionSpec as P

CELL_EDGE = 46.9
GRID = "grid"
UNROLL = 8


def basis(length):
    half = length // 2
    x = np.arange(length)
    rows = [np.full(length, 1.0 / math.sqrt(length))]
    rows += [math.sqrt(2.0 / length) * np.cos(2 * math.pi * (k * x % length) / length) for k in range(1, half)]
    rows += [(1.0 - 2.0 * (x % 2)) / math.sqrt(length)]
    rows += [math.sqrt(2.0 / length) * np.sin(2 * math.pi * (k * x % length) / length) for k in range(1, half)]
    return np.stack(rows)


def halves(table):
    table = table.astype(np.float32)
    high = table.astype(ml_dtypes.bfloat16)
    return high, (table - high.astype(np.float32)).astype(ml_dtypes.bfloat16)


def left_table(table):
    high, low = halves(table)
    return np.block([[high, high], [low, low]])


def right_table(table):
    high, low = halves(table)
    return np.block([[high, low], [high, low]])


def split(values):
    high = values.astype(jnp.bfloat16)
    return high, (values - high.astype(jnp.float32)).astype(jnp.bfloat16)


def from_left(table, values):
    product = jnp.dot(table, jnp.concatenate(split(values), axis=0), preferred_element_type=jnp.float32)
    rows = product.shape[0] // 2
    return product[:rows] + product[rows:]


def from_right(values, table):
    product = jnp.dot(jnp.concatenate(split(values), axis=1), table, preferred_element_type=jnp.float32)
    columns = product.shape[1] // 2
    return product[:, :columns] + product[:, columns:]


def outward(place_ref, core_ref, own_ref, mine_ref, other_ref, wz_ref, wy_ref, out_ref, chosen_ref):
    held, planes, ny, nz = own_ref.shape
    width = planes * held

    def one(r, carry):
        same = core_ref[r] == 0
        place = place_ref[r]
        done = []
        for p in range(planes):
            chosen = jnp.where(same, mine_ref[place, p], other_ref[place, p])
            chosen_ref[r, p] = chosen
            rho = jnp.concatenate([own_ref[i, p] * chosen for i in range(held)], axis=0)
            rho = from_right(rho, wz_ref[...])
            rho = jnp.concatenate([rho[i * ny:(i + 1) * ny] for i in range(held)], axis=1)
            rho = from_left(wy_ref[...], rho)
            done += [rho[:, i * nz:(i + 1) * nz] for i in range(held)]
        out_ref[:, pl.ds(pl.multiple_of(r * width, width), width), :] = jnp.swapaxes(jnp.stack(done), 0, 1)
        return carry

    lax.fori_loop(0, out_ref.shape[1] // width, one, 0, unroll=UNROLL)


def frequency(row, length):
    return jnp.where(row > length // 2, row - length // 2, row).astype(jnp.float32)


def middle(spot_ref, wx_ref, wxi_ref, in_ref, out_ref, kernel_ref):
    slabs, own_y, step, nz = in_ref.shape
    _, nx, _ = kernel_ref.shape
    held, planes = 2, nx // slabs
    width = planes * held
    scale = (2.0 * math.pi / CELL_EDGE) ** 2
    freq_x = frequency(lax.broadcasted_iota(jnp.int32, (nx, nz), 0), nx)
    freq_z = frequency(lax.broadcasted_iota(jnp.int32, (nx, nz), 1), nz)
    for q in range(own_y):
        freq_y = frequency(jnp.full((nx, nz), spot_ref[0] * own_y + q, jnp.int32), slabs * own_y)
        squared = scale * (freq_x**2 + freq_y**2 + freq_z**2)
        guarded = jnp.where(squared > 0, squared, 1.0)
        kernel_ref[q] = jnp.where(squared > 0, 4.0 * math.pi / guarded, 0.0)

    def one(r, carry):
        at = pl.ds(pl.multiple_of(r * width, width), width)
        for q in range(own_y):
            spec = jnp.swapaxes(in_ref[:, q, at, :], 0, 1).reshape(planes, held, slabs, nz)
            spec = jnp.concatenate([spec[:, i].reshape(planes * slabs, nz) for i in range(held)], axis=1)
            spec = from_left(wx_ref[...], spec)
            spec = spec * jnp.concatenate([kernel_ref[q]] * held, axis=1)
            spec = from_left(wxi_ref[...], spec)
            spec = jnp.stack([spec[:, i * nz:(i + 1) * nz].reshape(planes, slabs, nz) for i in range(held)], axis=1)
            out_ref[:, q, at, :] = jnp.swapaxes(spec.reshape(width, slabs, nz), 0, 1)
        return carry

    lax.fori_loop(0, step // width, one, 0, unroll=UNROLL)


def inward(in_ref, chosen_ref, wz_ref, wy_ref, out_ref):
    held, planes, ny, nz = out_ref.shape
    width = planes * held
    out_ref[...] = jnp.zeros_like(out_ref)

    def one(r, carry):
        pots = jnp.swapaxes(in_ref[:, pl.ds(pl.multiple_of(r * width, width), width), :], 0, 1)
        for p in range(planes):
            pot = jnp.concatenate([pots[p * held + i] for i in range(held)], axis=1)
            pot = from_left(wy_ref[...], pot)
            pot = jnp.concatenate([pot[:, i * nz:(i + 1) * nz] for i in range(held)], axis=0)
            pot = from_right(pot, wz_ref[...])
            for i in range(held):
                out_ref[i, p] -= chosen_ref[r, p] * pot[i * ny:(i + 1) * ny]
        return carry

    lax.fori_loop(0, in_ref.shape[1] // width, one, 0, unroll=UNROLL)


def rotated(array, axis, step):
    size = lax.axis_size(axis)
    return lax.ppermute(array, axis, [(i, (i + step) % size) for i in range(size)])


def every_orbital(own):
    held = own.shape[0] // 2
    first, last = own[:held], own[held:]
    below_first, above_last = rotated(first, "zh", 1), rotated(last, "zh", -1)
    below_last, above_first = rotated(last, "zh", 1), rotated(first, "zh", -1)
    far_first, far_last = rotated(below_first, "zh", 1), rotated(above_last, "zh", -1)
    blocks = [below_first, below_last, above_first, above_last]
    blocks.append(jnp.concatenate([far_first, far_last, own]))
    return jnp.concatenate(blocks), jnp.concatenate([rotated(block, "core", 1) for block in blocks])


def shards(orbitals, band_owner, block_index):
    held, planes, ny, nz = orbitals.shape
    rounds = band_owner.shape[0]
    grid = lax.axis_size(GRID)
    nx = planes * grid
    own_y = ny // grid
    width = planes * held
    tx, ty, tz = basis(nx), basis(ny), basis(nz)
    order = np.arange(grid).reshape(-1, 4, 4).transpose(2, 1, 0).reshape(grid)
    tx = tx.reshape(nx, grid, planes)[:, order].transpose(0, 2, 1).reshape(nx, nx)
    groups, cores = lax.axis_size("zh"), lax.axis_size("core")
    offset = (band_owner // cores - lax.axis_index("zh")) % groups
    place = jnp.where(offset == 0, groups - 1, jnp.where(offset == groups - 1, 0, offset)) * held + block_index
    core_off = (band_owner + lax.axis_index("core")) % cores

    here = lax.axis_index(GRID)
    spot = here % 4 * (grid // 4) + here // 4 % 4 * (grid // 16) + here // 16

    mine, other = every_orbital(orbitals)
    spot, other = lax.optimization_barrier((jnp.full((1,), spot, jnp.int32), other))
    cells = rounds * held * planes * ny * nz
    vmem, smem = pl.BlockSpec(memory_space=pltpu.VMEM), pl.BlockSpec(memory_space=pltpu.SMEM)

    def call(body, shapes, scalars, operands, scratch=()):
        return pl.pallas_call(
            body,
            in_specs=[smem] * len(scalars) + [vmem] * len(operands),
            out_specs=[vmem] * len(shapes),
            out_shape=[jax.ShapeDtypeStruct(shape, jnp.float32) for shape in shapes],
            scratch_shapes=scratch,
            compiler_params=pltpu.CompilerParams(vmem_limit_bytes=16 * 2**20),
            cost_estimate=pl.CostEstimate(flops=16 * nz * cells, bytes_accessed=8 * cells, transcendentals=0),
        )(*scalars, *operands)

    def exchange(array):
        return lax.all_to_all(
            array, GRID, split_axis=0, concat_axis=0, tiled=True, axis_index_groups=[order.tolist()]
        )

    sent = (ny, rounds * width, nz)
    half, chosen = call(
        outward,
        [sent, (rounds, planes, ny, nz)],
        (place, core_off),
        (orbitals, mine, other, right_table(tz.T), left_table(ty)),
    )
    strips = (grid, own_y, rounds * width, nz)
    spec = exchange(half).reshape(strips)
    (spec,) = call(
        middle,
        [strips],
        (spot,),
        (left_table(tx), left_table(tx.T), spec),
        [pltpu.VMEM((own_y, nx, nz), jnp.float32)],
    )
    half = exchange(spec.reshape(sent))
    (out,) = call(inward, [orbitals.shape], (), (half, chosen, right_table(tz), left_table(ty.T)))
    return out


def solution(mesh):
    parts = jax.sharding.Mesh(mesh.devices.reshape(4, 2, 32), ("zh", "core", GRID))
    placed = P(("zh", "core"), GRID, None, None)
    return jax.shard_map(
        shards,
        mesh=parts,
        in_specs=(placed, P(), P()),
        out_specs=placed,
        check_vma=False,
    )
```

```python
import math

import jax
import jax.numpy as jnp
import ml_dtypes
import numpy as np
from jax import lax
from jax.experimental import pallas as pl
from jax.experimental.pallas import tpu as pltpu
from jax.sharding import PartitionSpec as P

CELL_EDGE = 46.9
GRID = "grid"
UNROLL = 8


def basis(length):
    half = length // 2
    x = np.arange(length)
    rows = [np.full(length, 1.0 / math.sqrt(length))]
    rows += [math.sqrt(2.0 / length) * np.cos(2 * math.pi * (k * x % length) / length) for k in range(1, half)]
    rows += [(1.0 - 2.0 * (x % 2)) / math.sqrt(length)]
    rows += [math.sqrt(2.0 / length) * np.sin(2 * math.pi * (k * x % length) / length) for k in range(1, half)]
    return np.stack(rows)


def halves(table):
    table = table.astype(np.float32)
    high = table.astype(ml_dtypes.bfloat16)
    return high, (table - high.astype(np.float32)).astype(ml_dtypes.bfloat16)


def left_table(table):
    high, low = halves(table)
    return np.block([[high, high], [low, low]])


def right_table(table):
    high, low = halves(table)
    return np.block([[high, low], [high, low]])


def split(values):
    high = values.astype(jnp.bfloat16)
    return high, (values - high.astype(jnp.float32)).astype(jnp.bfloat16)


def from_left(table, values):
    product = jnp.dot(table, jnp.concatenate(split(values), axis=0), preferred_element_type=jnp.float32)
    rows = product.shape[0] // 2
    return product[:rows] + product[rows:]


def from_right(values, table):
    product = jnp.dot(jnp.concatenate(split(values), axis=1), table, preferred_element_type=jnp.float32)
    columns = product.shape[1] // 2
    return product[:, :columns] + product[:, columns:]


def outward(groups, cores, owner_ref, index_ref, own_ref, mine_ref, other_ref, wz_ref, wy_ref, out_ref, chosen_ref):
    held, planes, ny, nz = own_ref.shape
    width = planes * held

    def one(r, carry):
        owner = owner_ref[r]
        same = lax.rem(owner + lax.axis_index("core"), cores) == 0
        offset = lax.rem(lax.div(owner, cores) + groups - lax.axis_index("zh"), groups)
        place = jnp.where(offset == 0, groups - 1, jnp.where(offset == groups - 1, 0, offset)) * held + index_ref[r]
        done = []
        for p in range(planes):
            chosen = jnp.where(same, mine_ref[place, p], other_ref[place, p])
            chosen_ref[r, p] = chosen
            rho = jnp.concatenate([own_ref[i, p] * chosen for i in range(held)], axis=0)
            rho = from_right(rho, wz_ref[...])
            rho = jnp.concatenate([rho[i * ny:(i + 1) * ny] for i in range(held)], axis=1)
            rho = from_left(wy_ref[...], rho)
            done += [rho[:, i * nz:(i + 1) * nz] for i in range(held)]
        out_ref[:, pl.ds(pl.multiple_of(r * width, width), width), :] = jnp.swapaxes(jnp.stack(done), 0, 1)
        return carry

    lax.fori_loop(0, out_ref.shape[1] // width, one, 0, unroll=UNROLL)


def frequency(row, length):
    return jnp.where(row > length // 2, row - length // 2, row).astype(jnp.float32)


def middle(wx_ref, wxi_ref, in_ref, out_ref, kernel_ref):
    slabs, own_y, step, nz = in_ref.shape
    _, nx, _ = kernel_ref.shape
    held, planes = 2, nx // slabs
    width = planes * held
    here = lax.axis_index(GRID)
    spot = lax.rem(here, 4) * (slabs // 4) + lax.rem(lax.div(here, 4), 4) * (slabs // 16) + lax.div(here, 16)
    scale = (2.0 * math.pi / CELL_EDGE) ** 2
    freq_x = frequency(lax.broadcasted_iota(jnp.int32, (nx, nz), 0), nx)
    freq_z = frequency(lax.broadcasted_iota(jnp.int32, (nx, nz), 1), nz)
    for q in range(own_y):
        freq_y = frequency(jnp.full((nx, nz), spot * own_y + q, jnp.int32), slabs * own_y)
        squared = scale * (freq_x**2 + freq_y**2 + freq_z**2)
        guarded = jnp.where(squared > 0, squared, 1.0)
        kernel_ref[q] = jnp.where(squared > 0, 4.0 * math.pi / guarded, 0.0)

    def one(r, carry):
        at = pl.ds(pl.multiple_of(r * width, width), width)
        for q in range(own_y):
            spec = jnp.swapaxes(in_ref[:, q, at, :], 0, 1).reshape(planes, held, slabs, nz)
            spec = jnp.concatenate([spec[:, i].reshape(planes * slabs, nz) for i in range(held)], axis=1)
            spec = from_left(wx_ref[...], spec)
            spec = spec * jnp.concatenate([kernel_ref[q]] * held, axis=1)
            spec = from_left(wxi_ref[...], spec)
            spec = jnp.stack([spec[:, i * nz:(i + 1) * nz].reshape(planes, slabs, nz) for i in range(held)], axis=1)
            out_ref[:, q, at, :] = jnp.swapaxes(spec.reshape(width, slabs, nz), 0, 1)
        return carry

    lax.fori_loop(0, step // width, one, 0, unroll=UNROLL)


def inward(in_ref, chosen_ref, wz_ref, wy_ref, out_ref):
    held, planes, ny, nz = out_ref.shape
    width = planes * held
    out_ref[...] = jnp.zeros_like(out_ref)

    def one(r, carry):
        pots = jnp.swapaxes(in_ref[:, pl.ds(pl.multiple_of(r * width, width), width), :], 0, 1)
        for p in range(planes):
            pot = jnp.concatenate([pots[p * held + i] for i in range(held)], axis=1)
            pot = from_left(wy_ref[...], pot)
            pot = jnp.concatenate([pot[:, i * nz:(i + 1) * nz] for i in range(held)], axis=0)
            pot = from_right(pot, wz_ref[...])
            for i in range(held):
                out_ref[i, p] -= chosen_ref[r, p] * pot[i * ny:(i + 1) * ny]
        return carry

    lax.fori_loop(0, in_ref.shape[1] // width, one, 0, unroll=UNROLL)


def rotated(array, axis, step):
    size = lax.axis_size(axis)
    return lax.ppermute(array, axis, [(i, (i + step) % size) for i in range(size)])


def every_orbital(own):
    held = own.shape[0] // 2
    first, last = own[:held], own[held:]
    below_first, above_last = rotated(first, "zh", 1), rotated(last, "zh", -1)
    below_last, above_first = rotated(last, "zh", 1), rotated(first, "zh", -1)
    far_first, far_last = rotated(below_first, "zh", 1), rotated(above_last, "zh", -1)
    blocks = [below_first, below_last, above_first, above_last]
    blocks.append(jnp.concatenate([far_first, far_last, own]))
    return jnp.concatenate(blocks), jnp.concatenate([rotated(block, "core", 1) for block in blocks])


def shards(orbitals, band_owner, block_index):
    held, planes, ny, nz = orbitals.shape
    rounds = band_owner.shape[0]
    grid = lax.axis_size(GRID)
    nx = planes * grid
    own_y = ny // grid
    width = planes * held
    tx, ty, tz = basis(nx), basis(ny), basis(nz)
    order = np.arange(grid).reshape(-1, 4, 4).transpose(2, 1, 0).reshape(grid)
    tx = tx.reshape(nx, grid, planes)[:, order].transpose(0, 2, 1).reshape(nx, nx)
    groups, cores = lax.axis_size("zh"), lax.axis_size("core")
    mine, other = every_orbital(orbitals)
    cells = rounds * held * planes * ny * nz
    vmem, smem = pl.BlockSpec(memory_space=pltpu.VMEM), pl.BlockSpec(memory_space=pltpu.SMEM)

    def call(body, shapes, scalars, operands, scratch=()):
        return pl.pallas_call(
            body,
            in_specs=[smem] * len(scalars) + [vmem] * len(operands),
            out_specs=[vmem] * len(shapes),
            out_shape=[jax.ShapeDtypeStruct(shape, jnp.float32) for shape in shapes],
            scratch_shapes=scratch,
            compiler_params=pltpu.CompilerParams(vmem_limit_bytes=16 * 2**20),
            cost_estimate=pl.CostEstimate(flops=16 * nz * cells, bytes_accessed=8 * cells, transcendentals=0),
        )(*scalars, *operands)

    def exchange(array):
        return lax.all_to_all(
            array, GRID, split_axis=0, concat_axis=0, tiled=True, axis_index_groups=[order.tolist()]
        )

    sent = (ny, rounds * width, nz)
    half, chosen = call(
        lambda *refs: outward(groups, cores, *refs),
        [sent, (rounds, planes, ny, nz)],
        (band_owner, block_index),
        (orbitals, mine, other, right_table(tz.T), left_table(ty)),
    )
    strips = (grid, own_y, rounds * width, nz)
    spec = exchange(half).reshape(strips)
    (spec,) = call(
        middle,
        [strips],
        (),
        (left_table(tx), left_table(tx.T), spec),
        [pltpu.VMEM((own_y, nx, nz), jnp.float32)],
    )
    half = exchange(spec.reshape(sent))
    (out,) = call(inward, [orbitals.shape], (), (half, chosen, right_table(tz), left_table(ty.T)))
    return out


def solution(mesh):
    parts = jax.sharding.Mesh(mesh.devices.reshape(4, 2, 32), ("zh", "core", GRID))
    placed = P(("zh", "core"), GRID, None, None)
    return jax.shard_map(
        shards,
        mesh=parts,
        in_specs=(placed, P(), P()),
        out_specs=placed,
        check_vma=False,
    )
```
